32 devices in a mesh: frame: 8 (over y, x, core), row: 4 (over z).
Axes of the slice: x: 2, y: 2, z: 4, core: 2. Of those that a mesh axis runs over, the one named last changes fastest.
Arguments:
- clip: bfloat16 [16, 48, 128, 320], P('frame', 'row'), may hold values from -6 to 6
- w_spatial: bfloat16 [3, 3, 320, 320], replicated, may hold values from -0.109375 to 0.109375
- b_spatial: float32 [320], replicated, may hold values from -3 to 3
- w_temporal: bfloat16 [3, 320, 320], replicated, may hold values from -0.1875 to 0.1875
- b_temporal: float32 [320], replicated, may hold values from -3 to 3
- ln_gain: float32 [320], replicated, may hold values from 0.1 to 1.9
- ln_bias: float32 [320], replicated, may hold values from -3 to 3
- w_query: bfloat16 [320, 320], replicated, may hold values from -1.677051 to 1.677051
- w_key: bfloat16 [320, 320], replicated, may hold values from -1.677051 to 1.677051
- w_value: bfloat16 [320, 320], replicated, may hold values from -0.3125 to 0.3125
- w_out: bfloat16 [320, 320], replicated, may hold values from -0.3125 to 0.3125
- b_out: float32 [320], replicated, may hold values from -3 to 3
Outputs:
- mixed: bfloat16 [16, 48, 128, 320], P('frame', 'row')
The draws below stay inside these ranges and needn't reach their ends.
All inputs are finite; a program needn't handle non-finite values.
Results may differ from the reference program's by a relative error of at most 0.0062.
Values may be sent and summed in bfloat16 or wider, within the bound.
A program may use at most 128 MiB of HBM per device.

```python
import jax
import jax.numpy as jnp
from jax import lax

C = 320
HEAD = 64
HEADS = 5
COLS = 128
FRAMES = 16
ROWS = 48


def shared_projection(key, salt):
    own = jax.random.normal(jax.random.fold_in(key, salt), (C, C), jnp.float32)
    values = own / jnp.sqrt(jnp.float32(C))
    limit = 30.0 / jnp.sqrt(jnp.float32(C))
    return jnp.clip(values, -limit, limit).astype(jnp.bfloat16)


def draw_w_query(key, part):
    return shared_projection(key, 1)


def draw_w_key(key, part):
    return shared_projection(key, 2)


def shard_levels(own_key, shape, pieces, low, largest):
    level, own = 1.0, jax.random.fold_in(own_key, 6)
    for axis_at, blocks in pieces:
        heights = jnp.exp(jax.random.uniform(jax.random.fold_in(own, axis_at), (blocks,), jnp.float32, low / len(pieces), largest / len(pieces)))
        level = level * jnp.repeat(heights, shape[axis_at] // blocks).reshape([-1 if axis == axis_at else 1 for axis in range(len(shape))])
    return level


def centred(rng, shape, scale, reach, split=(), kind=jnp.bfloat16):
    entries = jax.random.normal(rng, shape, jnp.float32) * scale
    if len(split) > 0:
        entries = shard_levels(rng, shape, split, -0.22, 0.18) * entries
    return jnp.clip(entries, min=-reach, max=reach).astype(kind)


def setup_inputs(seed: int = 0) -> dict:
    splits = jax.random.split(jax.random.key(seed), 13)
    clip = centred(splits[0], (FRAMES, ROWS, COLS, C), 1.0, 6.0, ((0, 8), (1, 4)))
    w_spatial = centred(splits[1], (3, 3, C, C), (9 * C) ** -0.5, 0.109375)
    b_spatial = centred(splits[2], (C,), 0.5, 3.0, (), jnp.float32)
    w_temporal = centred(splits[3], (3, C, C), (3 * C) ** -0.5, 0.1875)
    b_temporal = centred(splits[4], (C,), 0.5, 3.0, (), jnp.float32)
    ln_gain = jnp.clip(1.0 + 0.18 * jax.random.normal(splits[5], (C,), jnp.float32), 0.1, 1.9)
    ln_bias = centred(splits[6], (C,), 0.5, 3.0, (), jnp.float32)
    w_query = draw_w_query(jax.random.fold_in(splits[12], 71), 0)
    w_key = draw_w_key(jax.random.fold_in(splits[12], 71), 0)
    w_value = centred(splits[9], (C, C), C ** -0.5, 0.3125)
    w_out = centred(splits[10], (C, C), C ** -0.5, 0.3125)
    b_out = centred(splits[11], (C,), 0.5, 3.0, (), jnp.float32)
    return {"clip": clip, "w_spatial": w_spatial, "b_spatial": b_spatial, "w_temporal": w_temporal, "b_temporal": b_temporal, "ln_gain": ln_gain, "ln_bias": ln_bias, "w_query": w_query, "w_key": w_key, "w_value": w_value, "w_out": w_out, "b_out": b_out}


def spatial_frame(frame, w_spatial, b_spatial):
    rows = frame.shape[0]
    cols = frame.shape[1]
    padded = jnp.pad(frame.astype(jnp.float32), ((1, 1), (1, 1), (0, 0)))
    weights = w_spatial.astype(jnp.float32)
    total = jnp.zeros((rows, cols, weights.shape[3]), jnp.float32) + b_spatial
    for tap_row in range(3):
        for tap_col in range(3):
            window = padded[tap_row:tap_row + rows, tap_col:tap_col + cols]
            total = total + jnp.einsum('rwc,co->rwo', window, weights[tap_row, tap_col])
    return total.astype(jnp.bfloat16)

def temporal_column(column, w_temporal, b_temporal, ln_gain, ln_bias, w_query, w_key, w_value, w_out, b_out):
    frames = column.shape[0]
    padded = jnp.pad(column.astype(jnp.float32), ((1, 1), (0, 0), (0, 0)))
    kernel = w_temporal.astype(jnp.float32)
    total = column.astype(jnp.float32) + b_temporal
    for tap in range(3):
        total = total + jnp.einsum('fwc,co->fwo', padded[tap:tap + frames], kernel[tap])
    framed = total.astype(jnp.bfloat16)
    values32 = framed.astype(jnp.float32)
    center = lax.optimization_barrier(jnp.mean(values32, axis=-1, keepdims=True))
    spread = lax.optimization_barrier(jnp.mean((values32 - center) ** 2, axis=-1, keepdims=True))
    normed = ((values32 - center) / jnp.sqrt(spread + 1e-05) * ln_gain + ln_bias).astype(jnp.bfloat16)
    normed32 = normed.astype(jnp.float32)
    query = jnp.einsum('fwc,cd->fwd', normed32, w_query.astype(jnp.float32)).astype(jnp.bfloat16)
    key = jnp.einsum('fwc,cd->fwd', normed32, w_key.astype(jnp.float32)).astype(jnp.bfloat16)
    value = jnp.einsum('fwc,cd->fwd', normed32, w_value.astype(jnp.float32)).astype(jnp.bfloat16)
    cols = column.shape[1]
    query = query.astype(jnp.float32).reshape(frames, cols, HEADS, HEAD)
    key = key.astype(jnp.float32).reshape(frames, cols, HEADS, HEAD)
    value = value.astype(jnp.float32).reshape(frames, cols, HEADS, HEAD)
    scores = jnp.einsum('fwhd,gwhd->whfg', query, key) / jnp.sqrt(jnp.float32(HEAD))
    top = lax.optimization_barrier(jnp.max(scores, axis=-1, keepdims=True))
    raised = jnp.exp(scores - top)
    weights = (raised / lax.optimization_barrier(jnp.sum(raised, axis=-1, keepdims=True))).astype(jnp.bfloat16)
    attended = jnp.einsum('whfg,gwhd->fwhd', weights.astype(jnp.float32), value)
    attended = attended.reshape(frames, cols, HEADS * HEAD).astype(jnp.bfloat16)
    result = values32 + jnp.einsum('fwc,co->fwo', attended.astype(jnp.float32), w_out.astype(jnp.float32)) + b_out
    return result.astype(jnp.bfloat16)

def reference(clip, w_spatial, b_spatial, w_temporal, b_temporal, ln_gain, ln_bias, w_query, w_key, w_value, w_out, b_out):
    spatial = lax.map(lambda frame: spatial_frame(frame, w_spatial, b_spatial), clip)
    by_rows = jnp.moveaxis(spatial, 1, 0)
    mixed = lax.map(lambda column: temporal_column(column, w_temporal, b_temporal, ln_gain, ln_bias, w_query, w_key, w_value, w_out, b_out), by_rows)
    return jnp.moveaxis(mixed, 0, 1)
```

```python
import functools

import jax
import jax.numpy as jnp
from jax import lax
from jax.experimental import pallas as pl
from jax.experimental.pallas import tpu as pltpu
from jax.sharding import PartitionSpec as P

HEAD = 64


def extended(block, sides, width):
    for axis, dim in sides:
        count = lax.axis_size(axis)
        forward = [(i, i + 1) for i in range(count - 1)]
        backward = [(target, source) for source, target in forward]
        low = lax.ppermute(
            lax.slice_in_dim(block, block.shape[dim] - width, None, axis=dim), axis, forward
        )
        high = lax.ppermute(lax.slice_in_dim(block, 0, width, axis=dim), axis, backward)
        block = jnp.concatenate([low, block, high], axis=dim)
    return block


def temporal_conv(padded, w_temporal, b_temporal):
    count = padded.shape[0] - 2
    total = padded[1 : 1 + count].astype(jnp.float32) + b_temporal
    for tap in range(3):
        total = total + jnp.einsum(
            "frwc,co->frwo",
            padded[tap : tap + count],
            w_temporal[tap],
            preferred_element_type=jnp.float32,
        )
    return total.astype(jnp.bfloat16)


def attend_back(framed, ln_gain, ln_bias, w_query, w_key, w_value, w_out, b_out):
    frames, rows, cols, width = framed.shape
    values32 = framed.astype(jnp.float32)
    center = jnp.mean(values32, axis=-1, keepdims=True)
    spread = jnp.mean((values32 - center) ** 2, axis=-1, keepdims=True)
    normed = ((values32 - center) * lax.rsqrt(spread + 1e-05) * ln_gain + ln_bias).astype(
        jnp.bfloat16
    )
    query = jnp.einsum("frwc,cd->frwd", normed, w_query, preferred_element_type=jnp.float32).astype(
        jnp.bfloat16
    )
    key_rows = jnp.einsum(
        "frwc,cd->frwd", normed, w_key, preferred_element_type=jnp.float32
    ).astype(jnp.bfloat16)
    value = jnp.einsum("frwc,cd->frwd", normed, w_value, preferred_element_type=jnp.float32).astype(
        jnp.bfloat16
    )
    heads = width // HEAD
    query = query.reshape(frames, rows, cols, heads, HEAD)
    key_rows = key_rows.reshape(frames, rows, cols, heads, HEAD)
    value = value.reshape(frames, rows, cols, heads, HEAD)
    scores = jnp.einsum(
        "frwhd,grwhd->rwhfg", query, key_rows, preferred_element_type=jnp.float32
    ) / jnp.sqrt(jnp.float32(HEAD))
    top = jnp.max(scores, axis=-1, keepdims=True)
    raised = jnp.exp(scores - top)
    weights = (raised / jnp.sum(raised, axis=-1, keepdims=True)).astype(jnp.bfloat16)
    attended = jnp.einsum("rwhfg,grwhd->frwhd", weights, value, preferred_element_type=jnp.float32)
    attended = attended.reshape(frames, rows, cols, width).astype(jnp.bfloat16)
    result = (
        values32
        + jnp.einsum("frwc,co->frwo", attended, w_out, preferred_element_type=jnp.float32)
        + b_out
    )
    result = result.astype(jnp.bfloat16)
    return lax.all_to_all(result, "frame", split_axis=0, concat_axis=2, tiled=True)


def on_device(
    clip,
    w_spatial,
    b_spatial,
    w_temporal,
    b_temporal,
    ln_gain,
    ln_bias,
    w_query,
    w_key,
    w_value,
    w_out,
    b_out,
):
    rows = clip.shape[1]
    cols = clip.shape[2]
    padded = extended(clip, (("row", 1),), 1)
    padded = jnp.pad(padded, ((0, 0), (0, 0), (1, 1), (0, 0)))
    total = jnp.zeros(clip.shape, jnp.float32) + b_spatial
    for tap_row in range(3):
        for tap_col in range(3):
            window = padded[:, tap_row : tap_row + rows, tap_col : tap_col + cols]
            total = total + jnp.einsum(
                "frwc,co->frwo",
                window,
                w_spatial[tap_row, tap_col],
                preferred_element_type=jnp.float32,
            )
    spatial = total.astype(jnp.bfloat16)
    zero_rim = jnp.pad(
        lax.all_to_all(spatial, "frame", split_axis=2, concat_axis=0, tiled=True),
        ((1, 1), (0, 0), (0, 0), (0, 0)),
    )
    framed = temporal_conv(zero_rim, w_temporal, b_temporal)
    return attend_back(framed, ln_gain, ln_bias, w_query, w_key, w_value, w_out, b_out)


MESH = pl.DeviceIdType.MESH
F32 = jnp.float32
BF16 = jnp.bfloat16
PARTS = 4


def down(x, count):
    return jnp.concatenate([jnp.zeros((count, x.shape[1]), x.dtype), x[:-count]], axis=0)


def up(x, count):
    return jnp.concatenate([x[count:], jnp.zeros((count, x.shape[1]), x.dtype)], axis=0)


def dot(a, b):
    return jnp.dot(a, b, preferred_element_type=F32)


def fused(
    n, nrow, clip, ws, bs, wt, bt, gain, lbias, wqkv, wo, bo, out,
    xp, snd, rcv, osnd, orcv, load_sem, hsend, hrecv, s1, r1, s2, r2,
):
    me = lax.axis_index("frame")
    zi = lax.axis_index("row")
    rows = clip.shape[1]
    per = rows // PARTS
    above = lax.rem(zi + 1, nrow)
    below = lax.rem(zi + nrow - 1, nrow)

    load = pltpu.make_async_copy(clip, xp.at[:, pl.ds(1, rows)], load_sem)
    load.start()

    barrier = pltpu.get_barrier_semaphore()

    def greet(k, _):
        pl.semaphore_signal(
            barrier, inc=1, device_id={"frame": lax.rem(me + k, n)}, device_id_type=MESH
        )
        return 0

    lax.fori_loop(1, n, greet, 0)
    pl.semaphore_signal(barrier, inc=1, device_id={"row": above}, device_id_type=MESH)
    pl.semaphore_signal(barrier, inc=1, device_id={"row": below}, device_id_type=MESH)
    pl.semaphore_wait(barrier, n + 1)

    to_above = pltpu.make_async_remote_copy(
        src_ref=clip.at[:, rows - 1], dst_ref=xp.at[:, 0],
        send_sem=hsend.at[0], recv_sem=hrecv.at[0],
        device_id={"row": above}, device_id_type=MESH,
    )
    to_below = pltpu.make_async_remote_copy(
        src_ref=clip.at[:, 0], dst_ref=xp.at[:, rows + 1],
        send_sem=hsend.at[1], recv_sem=hrecv.at[1],
        device_id={"row": below}, device_id_type=MESH,
    )
    to_above.start()
    to_below.start()
    load.wait()

    def move(buf, land, ss, rs, part, k):
        peer = lax.rem(me + k, n)
        span = pl.ds(part * per, per)
        return pltpu.make_async_remote_copy(
            src_ref=buf.at[peer, span], dst_ref=land.at[me, span],
            send_sem=ss.at[part, k], recv_sem=rs.at[part, k],
            device_id={"frame": peer}, device_id_type=MESH,
        )

    def arrived(buf, land, ss, rs, part, k):
        source = lax.rem(me + n - k, n)
        span = pl.ds(part * per, per)
        return pltpu.make_async_remote_copy(
            src_ref=buf.at[source, span], dst_ref=land.at[source, span],
            send_sem=ss.at[part, k], recv_sem=rs.at[part, k],
            device_id={"frame": source}, device_id_type=MESH,
        )

    def send_all(buf, land, ss, rs, part):
        def one(k, _):
            move(buf, land, ss, rs, part, k).start()
            return 0
        lax.fori_loop(1, n, one, 0)
        span = pl.ds(part * per, per)
        land[me, span] = buf[me, span]

    def recv_all(buf, land, ss, rs, part):
        def one(k, _):
            arrived(buf, land, ss, rs, part, k).wait_recv()
            return 0
        lax.fori_loop(1, n, one, 0)

    def drain(buf, land, ss, rs):
        def one(i, _):
            move(buf, land, ss, rs, i // (n - 1), 1 + i % (n - 1)).wait_send()
            return 0
        lax.fori_loop(0, PARTS * (n - 1), one, 0)

    def taps(y):
        main = [y[:, 256 * b : 256 * b + 256] for b in range(3)]
        left = [y[:, 768 + 64 * b : 832 + 64 * b] for b in range(3)]
        return main, left

    def conv_row(r):
        x = [xp[:, r + a].reshape(256, 320) for a in range(3)]
        y = dot(jnp.concatenate(x, axis=1), ws[...])
        pieces = []
        for f in range(2):
            main, left = taps(y[128 * f : 128 * f + 128])
            pieces.append([
                down(t[0], 1) + t[1] + up(t[2], 1) + b
                for t, b in ((main, bs[:, :256]), (left, bs[:, 256:]))
            ])

        def grouped(values):
            width = values[0].shape[1]
            both = [v.reshape(n, 2, 1, 8, width) for v in values]
            return [
                jnp.concatenate([both[0][:, g], both[1][:, g]], axis=1).reshape(n, 16, width)
                for g in range(2)
            ]

        main = grouped([pieces[0][0], pieces[1][0]])
        left = grouped([pieces[0][1], pieces[1][1]])
        for g in range(2):
            for half in range(2):
                snd[:, r, 2 * g + half] = main[g][:, :, 128 * half : 128 * half + 128].astype(BF16)
        snd[:, r, 4] = jnp.concatenate(left, axis=2).astype(BF16)

    lane = lax.broadcasted_iota(jnp.int32, (1, 128), 1)
    low = lane < HEAD
    same = lax.broadcasted_iota(jnp.int32, (8, 128), 0) == lax.broadcasted_iota(
        jnp.int32, (8, 128), 1
    ) % 8
    wall = jnp.where(same, 0.0, -1e30).astype(F32)

    def attend_row(r):
        m = 16 * n
        rest = rcv[:, r, 4].reshape(m, 128).astype(F32)
        xs = []
        for g in range(2):
            a = rcv[:, r, 2 * g].reshape(m, 128).astype(F32)
            b = rcv[:, r, 2 * g + 1].reshape(m, 128).astype(F32)
            own = rest if g == 0 else pltpu.roll(rest, 64, 1)
            xs.append(jnp.concatenate([a, b, own[:, :64]], axis=1))
        x = jnp.concatenate(xs, axis=0)
        y = dot(x.astype(BF16), wt[...])
        sums = []
        for g in range(2):
            main, left = taps(y[m * g : m * g + m])
            sums.append(jnp.concatenate(
                [down(t[0], 8) + t[1] + up(t[2], 8) for t in (main, left)], axis=1
            ))
        framed = (x + bt[...] + jnp.concatenate(sums, axis=0)).astype(BF16).astype(F32)
        center = jnp.sum(framed, axis=1, keepdims=True) * (1.0 / framed.shape[1])
        away = framed - center
        spread = jnp.sum(away * away, axis=1, keepdims=True) * (1.0 / framed.shape[1])
        normed = (away * lax.rsqrt(spread + 1e-05) * gain[...] + lbias[...]).astype(BF16)
        qkv = dot(normed, wqkv[...])
        ones = jnp.ones((m, 128), BF16)
        rows_out = []
        for g in range(2):
            part = qkv[m * g : m * g + m]

            def head(q, k, v):
                s = lax.dot_general(
                    q.astype(BF16), k, (((1,), (1,)), ((), ())), preferred_element_type=F32
                )
                s = (s.reshape(m // 8, 8, m) + wall[None]).reshape(m, m)
                e = jnp.exp(s - jnp.max(s, axis=1, keepdims=True)).astype(BF16)
                return dot(e, jnp.concatenate([v, ones], axis=1))

            cols = []
            for j in range(2):
                q = part[:, 128 * j : 128 * j + 128]
                k = part[:, 256 + 128 * j : 384 + 128 * j].astype(BF16)
                v = part[:, 512 + 128 * j : 640 + 128 * j].astype(BF16)
                even = head(jnp.where(low, q, 0.0), k, v)
                odd = head(jnp.where(low, 0.0, q), k, v)
                cols.append(
                    (jnp.where(low, even[:, :128], odd[:, :128])
                     / jnp.where(low, even[:, 128:], odd[:, 128:])).astype(BF16)
                )
            kv = part[:, 896:1024].astype(BF16)
            last = head(part[:, 768:896], kv, kv)
            cols.append((last[:, :128] / last[:, 128:]).astype(BF16))
            rows_out.append(jnp.concatenate(cols, axis=1))
        result = framed + dot(jnp.concatenate(rows_out, axis=0), wo[...]) + bo[...]
        lefts = []
        for g in range(2):
            part = result[m * g : m * g + m]
            for half in range(2):
                osnd[:, r, 2 * g + half] = (
                    part[:, 128 * half : 128 * half + 128].astype(BF16).reshape(n, 16, 128)
                )
            lefts.append(part[:, 256:])
        osnd[:, r, 4] = jnp.concatenate(lefts, axis=1).astype(BF16).reshape(n, 16, 128)

    def unpack_row(r):
        def pair(first, second):
            a = first.reshape(n, 2, 8, 128)
            b = second.reshape(n, 2, 8, 128)
            return [
                jnp.concatenate([a[:, f : f + 1], b[:, f : f + 1]], axis=1).reshape(16 * n, 128)
                for f in range(2)
            ]

        block = [orcv[:, r, i].astype(F32).reshape(16 * n, 128) for i in range(5)]
        for half in range(2):
            for f, value in enumerate(pair(block[half], block[2 + half])):
                out[f, r, :, 128 * half : 128 * half + 128] = value.astype(BF16)
        for f, value in enumerate(pair(block[4], pltpu.roll(block[4], 64, 1))):
            out[f, r, :, 256:320] = value[:, :64].astype(BF16)

    def each_row(part, body):
        def one(i, _):
            body(part * per + i)
            return 0
        lax.fori_loop(0, per, one, 0)

    def conv_part(i, _):
        part = lax.rem(i + 1, PARTS)

        @pl.when(i == PARTS - 2)
        def _():
            to_above.wait()
            to_below.wait()

            @pl.when(zi == 0)
            def _():
                xp[:, 0] = jnp.zeros((2,) + xp.shape[2:], BF16)

            @pl.when(zi == nrow - 1)
            def _():
                xp[:, rows + 1] = jnp.zeros((2,) + xp.shape[2:], BF16)

        each_row(part, conv_row)
        send_all(snd, rcv, s1, r1, part)
        return 0

    lax.fori_loop(0, PARTS, conv_part, 0)

    def attend_part(i, _):
        part = lax.rem(i + 1, PARTS)
        recv_all(snd, rcv, s1, r1, part)
        each_row(part, attend_row)
        send_all(osnd, orcv, s2, r2, part)
        return 0

    lax.fori_loop(0, PARTS, attend_part, 0)

    def unpack_part(i, _):
        part = lax.rem(i + 1, PARTS)
        recv_all(osnd, orcv, s2, r2, part)
        each_row(part, unpack_row)
        return 0

    lax.fori_loop(0, PARTS, unpack_part, 0)
    drain(snd, rcv, s1, r1)
    drain(osnd, orcv, s2, r2)


def taps_first(taps):
    return jnp.concatenate([t[:, :256] for t in taps] + [t[:, 256:] for t in taps], axis=1)


def fused_call(
    n, nrow, clip, w_spatial, b_spatial, w_temporal, b_temporal,
    ln_gain, ln_bias, w_query, w_key, w_value, w_out, b_out,
):
    width = clip.shape[3]
    rows = clip.shape[1]
    ws = taps_first([w_spatial[:, b].reshape(3 * width, width) for b in range(3)])
    wt = taps_first([w_temporal[k] for k in range(3)])
    wq = w_query * jnp.asarray(HEAD ** -0.5, BF16)
    wqkv = jnp.concatenate(
        [wq[:, :256], w_key[:, :256], w_value[:, :256], wq[:, 256:],
         jnp.zeros((width, 64), BF16), w_key[:, 256:], w_value[:, 256:]], axis=1,
    )
    wo = jnp.concatenate([w_out[:256], jnp.zeros((64, width), BF16), w_out[256:]], axis=0)
    vmem = pl.BlockSpec(memory_space=pltpu.VMEM)
    box = pltpu.VMEM((n, rows, 5, 16, 128), BF16)
    sems = pltpu.SemaphoreType.DMA((PARTS, n))
    return pl.pallas_call(
        functools.partial(fused, n, nrow),
        out_shape=jax.ShapeDtypeStruct(clip.shape, BF16),
        in_specs=[pl.BlockSpec(memory_space=pl.ANY)] + [vmem] * 9,
        out_specs=vmem,
        scratch_shapes=[
            pltpu.VMEM((2, rows + 2) + clip.shape[2:], BF16),
            box, box, box, box,
            pltpu.SemaphoreType.DMA,
            pltpu.SemaphoreType.DMA((2,)),
            pltpu.SemaphoreType.DMA((2,)),
            sems, sems, sems, sems,
        ],
        compiler_params=pltpu.CompilerParams(
            collective_id=0, has_side_effects=True, vmem_limit_bytes=48 * 1024 * 1024
        ),
        cost_estimate=pl.CostEstimate(
            flops=2 * 16 * width * width * clip.size // width,
            bytes_accessed=4 * clip.size, transcendentals=0,
        ),
    )(
        clip, ws, b_spatial[None], wt, b_temporal[None], ln_gain[None], ln_bias[None],
        wqkv, wo, b_out[None],
    )


def solution(mesh):
    n, nrow = mesh.shape["frame"], mesh.shape["row"]

    def body(clip, *weights):
        frames, rows, cols, width = clip.shape
        if (frames, cols, width, n) == (2, 128, 5 * HEAD, 8) and rows % PARTS == 0 and nrow > 2:
            return fused_call(n, nrow, clip, *weights)
        return on_device(clip, *weights)

    placed = (P("frame", "row", None, None), P(), P(), P(), P(), P(), P(), P(), P(), P(), P(), P())
    return jax.shard_map(
        body,
        mesh=mesh,
        in_specs=placed,
        out_specs=P("frame", "row", None, None),
        check_vma=False,
    )
```

```python
import functools

import jax
import jax.numpy as jnp
from jax import lax
from jax.experimental import pallas as pl
from jax.experimental.pallas import tpu as pltpu
from jax.sharding import PartitionSpec as P

HEAD = 64


def extended(block, sides, width):
    for axis, dim in sides:
        count = lax.axis_size(axis)
        forward = [(i, i + 1) for i in range(count - 1)]
        backward = [(target, source) for source, target in forward]
        low = lax.ppermute(
            lax.slice_in_dim(block, block.shape[dim] - width, None, axis=dim), axis, forward
        )
        high = lax.ppermute(lax.slice_in_dim(block, 0, width, axis=dim), axis, backward)
        block = jnp.concatenate([low, block, high], axis=dim)
    return block


def temporal_conv(padded, w_temporal, b_temporal):
    count = padded.shape[0] - 2
    total = padded[1 : 1 + count].astype(jnp.float32) + b_temporal
    for tap in range(3):
        total = total + jnp.einsum(
            "frwc,co->frwo",
            padded[tap : tap + count],
            w_temporal[tap],
            preferred_element_type=jnp.float32,
        )
    return total.astype(jnp.bfloat16)


def attend_back(framed, ln_gain, ln_bias, w_query, w_key, w_value, w_out, b_out):
    frames, rows, cols, width = framed.shape
    values32 = framed.astype(jnp.float32)
    center = jnp.mean(values32, axis=-1, keepdims=True)
    spread = jnp.mean((values32 - center) ** 2, axis=-1, keepdims=True)
    normed = ((values32 - center) * lax.rsqrt(spread + 1e-05) * ln_gain + ln_bias).astype(
        jnp.bfloat16
    )
    query = jnp.einsum("frwc,cd->frwd", normed, w_query, preferred_element_type=jnp.float32).astype(
        jnp.bfloat16
    )
    key_rows = jnp.einsum(
        "frwc,cd->frwd", normed, w_key, preferred_element_type=jnp.float32
    ).astype(jnp.bfloat16)
    value = jnp.einsum("frwc,cd->frwd", normed, w_value, preferred_element_type=jnp.float32).astype(
        jnp.bfloat16
    )
    heads = width // HEAD
    query = query.reshape(frames, rows, cols, heads, HEAD)
    key_rows = key_rows.reshape(frames, rows, cols, heads, HEAD)
    value = value.reshape(frames, rows, cols, heads, HEAD)
    scores = jnp.einsum(
        "frwhd,grwhd->rwhfg", query, key_rows, preferred_element_type=jnp.float32
    ) / jnp.sqrt(jnp.float32(HEAD))
    top = jnp.max(scores, axis=-1, keepdims=True)
    raised = jnp.exp(scores - top)
    weights = (raised / jnp.sum(raised, axis=-1, keepdims=True)).astype(jnp.bfloat16)
    attended = jnp.einsum("rwhfg,grwhd->frwhd", weights, value, preferred_element_type=jnp.float32)
    attended = attended.reshape(frames, rows, cols, width).astype(jnp.bfloat16)
    result = (
        values32
        + jnp.einsum("frwc,co->frwo", attended, w_out, preferred_element_type=jnp.float32)
        + b_out
    )
    result = result.astype(jnp.bfloat16)
    return lax.all_to_all(result, "frame", split_axis=0, concat_axis=2, tiled=True)


def on_device(
    clip,
    w_spatial,
    b_spatial,
    w_temporal,
    b_temporal,
    ln_gain,
    ln_bias,
    w_query,
    w_key,
    w_value,
    w_out,
    b_out,
):
    rows = clip.shape[1]
    cols = clip.shape[2]
    padded = extended(clip, (("row", 1),), 1)
    padded = jnp.pad(padded, ((0, 0), (0, 0), (1, 1), (0, 0)))
    total = jnp.zeros(clip.shape, jnp.float32) + b_spatial
    for tap_row in range(3):
        for tap_col in range(3):
            window = padded[:, tap_row : tap_row + rows, tap_col : tap_col + cols]
            total = total + jnp.einsum(
                "frwc,co->frwo",
                window,
                w_spatial[tap_row, tap_col],
                preferred_element_type=jnp.float32,
            )
    spatial = total.astype(jnp.bfloat16)
    zero_rim = jnp.pad(
        lax.all_to_all(spatial, "frame", split_axis=2, concat_axis=0, tiled=True),
        ((1, 1), (0, 0), (0, 0), (0, 0)),
    )
    framed = temporal_conv(zero_rim, w_temporal, b_temporal)
    return attend_back(framed, ln_gain, ln_bias, w_query, w_key, w_value, w_out, b_out)


MESH = pl.DeviceIdType.MESH
F32 = jnp.float32
BF16 = jnp.bfloat16
PARTS = 4


def down(x, count):
    return jnp.concatenate([jnp.zeros((count, x.shape[1]), x.dtype), x[:-count]], axis=0)


def up(x, count):
    return jnp.concatenate([x[count:], jnp.zeros((count, x.shape[1]), x.dtype)], axis=0)


def dot(a, b):
    return jnp.dot(a, b, preferred_element_type=F32)


def fused(
    n, nrow, clip, wsp, wtp, wq, wk, wv, wo_in, vecs, out,
    ws, wt, wqkv, wo, xp, snd, rcv, osnd, orcv, load_sem, hsend, hrecv, s1, r1, s2, r2,
):
    me = lax.axis_index("frame")
    zi = lax.axis_index("row")
    rows = clip.shape[1]
    per = rows // PARTS
    above = lax.rem(zi + 1, nrow)
    below = lax.rem(zi + nrow - 1, nrow)

    load = pltpu.make_async_copy(clip, xp.at[:, pl.ds(1, rows)], load_sem)
    load.start()
    bs, bt, gain, lbias, bo = [vecs.at[pl.ds(i, 1)] for i in range(5)]

    barrier = pltpu.get_barrier_semaphore()

    def greet(k, _):
        pl.semaphore_signal(
            barrier, inc=1, device_id={"frame": lax.rem(me + k, n)}, device_id_type=MESH
        )
        return 0

    lax.fori_loop(1, n, greet, 0)
    pl.semaphore_signal(barrier, inc=1, device_id={"row": above}, device_id_type=MESH)
    pl.semaphore_signal(barrier, inc=1, device_id={"row": below}, device_id_type=MESH)
    pl.semaphore_wait(barrier, n + 1)

    to_above = pltpu.make_async_remote_copy(
        src_ref=clip.at[:, rows - 1], dst_ref=xp.at[:, 0],
        send_sem=hsend.at[0], recv_sem=hrecv.at[0],
        device_id={"row": above}, device_id_type=MESH,
    )
    to_below = pltpu.make_async_remote_copy(
        src_ref=clip.at[:, 0], dst_ref=xp.at[:, rows + 1],
        send_sem=hsend.at[1], recv_sem=hrecv.at[1],
        device_id={"row": below}, device_id_type=MESH,
    )
    to_above.start()
    to_below.start()

    def lay(target, first, count, parts):
        for b, w in enumerate(parts):
            target[first : first + count, 256 * b : 256 * b + 256] = w[:, :256]
        left = [w[:, 256:].astype(F32) for w in parts]
        target[first : first + count, 768:896] = jnp.concatenate(left[:2], axis=1).astype(BF16)
        target[first : first + count, 896:960] = left[2].astype(BF16)

    width = wq.shape[0]
    for a in range(3):
        lay(ws, width * a, width, [wsp[a, b] for b in range(3)])
    lay(wt, 0, width, [wtp[k] for k in range(3)])
    scaled = (wq[...].astype(F32) * HEAD ** -0.5).astype(BF16)
    wqkv[:, :256] = scaled[:, :256]
    wqkv[:, 256:512] = wk[:, :256]
    wqkv[:, 512:768] = wv[:, :256]
    wqkv[:, 768:896] = jnp.concatenate(
        [scaled[:, 256:].astype(F32), jnp.zeros((width, 64), F32)], axis=1
    ).astype(BF16)
    wqkv[:, 896:1024] = jnp.concatenate(
        [wk[:, 256:].astype(F32), wv[:, 256:].astype(F32)], axis=1
    ).astype(BF16)
    wo[:256] = wo_in[:256]
    wo[256:320] = jnp.zeros((64, width), BF16)
    wo[320:] = wo_in[256:]
    load.wait()

    def move(buf, land, ss, rs, part, k):
        peer = lax.rem(me + k, n)
        span = pl.ds(part * per, per)
        return pltpu.make_async_remote_copy(
            src_ref=buf.at[peer, span], dst_ref=land.at[me, span],
            send_sem=ss.at[part, k], recv_sem=rs.at[part, k],
            device_id={"frame": peer}, device_id_type=MESH,
        )

    def arrived(buf, land, ss, rs, part, k):
        source = lax.rem(me + n - k, n)
        span = pl.ds(part * per, per)
        return pltpu.make_async_remote_copy(
            src_ref=buf.at[source, span], dst_ref=land.at[source, span],
            send_sem=ss.at[part, k], recv_sem=rs.at[part, k],
            device_id={"frame": source}, device_id_type=MESH,
        )

    def send_all(buf, land, ss, rs, part):
        def one(k, _):
            move(buf, land, ss, rs, part, k).start()
            return 0
        lax.fori_loop(1, n, one, 0)
        span = pl.ds(part * per, per)
        land[me, span] = buf[me, span]

    def recv_all(buf, land, ss, rs, part):
        def one(k, _):
            arrived(buf, land, ss, rs, part, k).wait_recv()
            return 0
        lax.fori_loop(1, n, one, 0)

    def drain(buf, land, ss, rs):
        def one(i, _):
            move(buf, land, ss, rs, i // (n - 1), 1 + i % (n - 1)).wait_send()
            return 0
        lax.fori_loop(0, PARTS * (n - 1), one, 0)

    def taps(y):
        main = [y[:, 256 * b : 256 * b + 256] for b in range(3)]
        left = [y[:, 768 + 64 * b : 832 + 64 * b] for b in range(3)]
        return main, left

    def conv_row(r):
        x = [xp[:, r + a].reshape(256, 320) for a in range(3)]
        y = dot(jnp.concatenate(x, axis=1), ws[...])
        pieces = []
        for f in range(2):
            main, left = taps(y[128 * f : 128 * f + 128])
            pieces.append([
                down(t[0], 1) + t[1] + up(t[2], 1) + b
                for t, b in ((main, bs[...][:, :256]), (left, bs[...][:, 256:]))
            ])

        def grouped(values):
            width = values[0].shape[1]
            both = [v.reshape(n, 2, 1, 8, width) for v in values]
            return [
                jnp.concatenate([both[0][:, g], both[1][:, g]], axis=1).reshape(n, 16, width)
                for g in range(2)
            ]

        main = grouped([pieces[0][0], pieces[1][0]])
        left = grouped([pieces[0][1], pieces[1][1]])
        for g in range(2):
            for half in range(2):
                snd[:, r, 2 * g + half] = main[g][:, :, 128 * half : 128 * half + 128].astype(BF16)
        snd[:, r, 4] = jnp.concatenate(left, axis=2).astype(BF16)

    lane = lax.broadcasted_iota(jnp.int32, (1, 128), 1)
    low = lane < HEAD
    same = lax.broadcasted_iota(jnp.int32, (8, 128), 0) == lax.broadcasted_iota(
        jnp.int32, (8, 128), 1
    ) % 8
    wall = jnp.where(same, 0.0, -1e30).astype(F32)

    def attend_row(r):
        m = 16 * n
        rest = rcv[:, r, 4].reshape(m, 128).astype(F32)
        xs = []
        for g in range(2):
            a = rcv[:, r, 2 * g].reshape(m, 128).astype(F32)
            b = rcv[:, r, 2 * g + 1].reshape(m, 128).astype(F32)
            own = rest if g == 0 else pltpu.roll(rest, 64, 1)
            xs.append(jnp.concatenate([a, b, own[:, :64]], axis=1))
        x = jnp.concatenate(xs, axis=0)
        y = dot(x.astype(BF16), wt[...])
        sums = []
        for g in range(2):
            main, left = taps(y[m * g : m * g + m])
            sums.append(jnp.concatenate(
                [down(t[0], 8) + t[1] + up(t[2], 8) for t in (main, left)], axis=1
            ))
        framed = (x + bt[...] + jnp.concatenate(sums, axis=0)).astype(BF16).astype(F32)
        center = jnp.sum(framed, axis=1, keepdims=True) * (1.0 / framed.shape[1])
        away = framed - center
        spread = jnp.sum(away * away, axis=1, keepdims=True) * (1.0 / framed.shape[1])
        normed = (away * lax.rsqrt(spread + 1e-05) * gain[...] + lbias[...]).astype(BF16)
        qkv = dot(normed, wqkv[...])
        ones = jnp.ones((m, 128), BF16)
        rows_out = []
        for g in range(2):
            part = qkv[m * g : m * g + m]

            def head(q, k, v):
                s = lax.dot_general(
                    q.astype(BF16), k, (((1,), (1,)), ((), ())), preferred_element_type=F32
                )
                s = (s.reshape(m // 8, 8, m) + wall[None]).reshape(m, m)
                e = jnp.exp(s - jnp.max(s, axis=1, keepdims=True)).astype(BF16)
                return dot(e, jnp.concatenate([v, ones], axis=1))

            cols = []
            for j in range(2):
                q = part[:, 128 * j : 128 * j + 128]
                k = part[:, 256 + 128 * j : 384 + 128 * j].astype(BF16)
                v = part[:, 512 + 128 * j : 640 + 128 * j].astype(BF16)
                even = head(jnp.where(low, q, 0.0), k, v)
                odd = head(jnp.where(low, 0.0, q), k, v)
                cols.append(
                    (jnp.where(low, even[:, :128], odd[:, :128])
                     / jnp.where(low, even[:, 128:], odd[:, 128:])).astype(BF16)
                )
            kv = part[:, 896:1024].astype(BF16)
            last = head(part[:, 768:896], kv, kv)
            cols.append((last[:, :128] / last[:, 128:]).astype(BF16))
            rows_out.append(jnp.concatenate(cols, axis=1))
        result = framed + dot(jnp.concatenate(rows_out, axis=0), wo[...]) + bo[...]
        lefts = []
        for g in range(2):
            part = result[m * g : m * g + m]
            for half in range(2):
                osnd[:, r, 2 * g + half] = (
                    part[:, 128 * half : 128 * half + 128].astype(BF16).reshape(n, 16, 128)
                )
            lefts.append(part[:, 256:])
        osnd[:, r, 4] = jnp.concatenate(lefts, axis=1).astype(BF16).reshape(n, 16, 128)

    def unpack_row(r):
        def pair(first, second):
            a = first.reshape(n, 2, 8, 128)
            b = second.reshape(n, 2, 8, 128)
            return [
                jnp.concatenate([a[:, f : f + 1], b[:, f : f + 1]], axis=1).reshape(16 * n, 128)
                for f in range(2)
            ]

        block = [orcv[:, r, i].astype(F32).reshape(16 * n, 128) for i in range(5)]
        for half in range(2):
            for f, value in enumerate(pair(block[half], block[2 + half])):
                out[f, r, :, 128 * half : 128 * half + 128] = value.astype(BF16)
        for f, value in enumerate(pair(block[4], pltpu.roll(block[4], 64, 1))):
            out[f, r, :, 256:320] = value[:, :64].astype(BF16)

    def each_row(part, body):
        def one(i, _):
            body(part * per + i)
            return 0
        lax.fori_loop(0, per, one, 0)

    def conv_part(i, _):
        part = lax.rem(i + 1, PARTS)

        @pl.when(i == PARTS - 2)
        def _():
            to_above.wait()
            to_below.wait()

            @pl.when(zi == 0)
            def _():
                xp[:, 0] = jnp.zeros((2,) + xp.shape[2:], BF16)

            @pl.when(zi == nrow - 1)
            def _():
                xp[:, rows + 1] = jnp.zeros((2,) + xp.shape[2:], BF16)

        each_row(part, conv_row)
        send_all(snd, rcv, s1, r1, part)
        return 0

    lax.fori_loop(0, PARTS, conv_part, 0)

    def attend_part(i, _):
        part = lax.rem(i + 1, PARTS)
        recv_all(snd, rcv, s1, r1, part)
        each_row(part, attend_row)
        send_all(osnd, orcv, s2, r2, part)
        return 0

    lax.fori_loop(0, PARTS, attend_part, 0)

    def unpack_part(i, _):
        part = lax.rem(i + 1, PARTS)
        recv_all(osnd, orcv, s2, r2, part)
        each_row(part, unpack_row)
        return 0

    lax.fori_loop(0, PARTS, unpack_part, 0)
    drain(snd, rcv, s1, r1)
    drain(osnd, orcv, s2, r2)


def fused_call(
    n, nrow, clip, w_spatial, b_spatial, w_temporal, b_temporal,
    ln_gain, ln_bias, w_query, w_key, w_value, w_out, b_out,
):
    width = clip.shape[3]
    rows = clip.shape[1]
    vecs = jnp.stack([b_spatial, b_temporal, ln_gain, ln_bias, b_out])
    vmem = pl.BlockSpec(memory_space=pltpu.VMEM)
    box = pltpu.VMEM((n, rows, 5, 16, 128), BF16)
    sems = pltpu.SemaphoreType.DMA((PARTS, n))
    return pl.pallas_call(
        functools.partial(fused, n, nrow),
        out_shape=jax.ShapeDtypeStruct(clip.shape, BF16),
        in_specs=[pl.BlockSpec(memory_space=pl.ANY)] + [vmem] * 7,
        out_specs=vmem,
        scratch_shapes=[
            pltpu.VMEM((3 * width, 3 * width), BF16),
            pltpu.VMEM((width, 3 * width), BF16),
            pltpu.VMEM((width, 3 * width + 64), BF16),
            pltpu.VMEM((width + 64, width), BF16),
            pltpu.VMEM((2, rows + 2) + clip.shape[2:], BF16),
            box, box, box, box,
            pltpu.SemaphoreType.DMA,
            pltpu.SemaphoreType.DMA((2,)),
            pltpu.SemaphoreType.DMA((2,)),
            sems, sems, sems, sems,
        ],
        compiler_params=pltpu.CompilerParams(
            collective_id=0, has_side_effects=True, vmem_limit_bytes=48 * 1024 * 1024
        ),
        cost_estimate=pl.CostEstimate(
            flops=2 * 16 * width * width * clip.size // width,
            bytes_accessed=4 * clip.size, transcendentals=0,
        ),
    )(
        clip, w_spatial, w_temporal, w_query, w_key, w_value, w_out, vecs,
    )


def solution(mesh):
    n, nrow = mesh.shape["frame"], mesh.shape["row"]

    def body(clip, *weights):
        frames, rows, cols, width = clip.shape
        if (frames, cols, width, n) == (2, 128, 5 * HEAD, 8) and rows % PARTS == 0 and nrow > 2:
            return fused_call(n, nrow, clip, *weights)
        return on_device(clip, *weights)

    placed = (P("frame", "row", None, None), P(), P(), P(), P(), P(), P(), P(), P(), P(), P(), P())
    return jax.shard_map(
        body,
        mesh=mesh,
        in_specs=placed,
        out_specs=P("frame", "row", None, None),
        check_vma=False,
    )
```

```python
import functools

import jax
import jax.numpy as jnp
from jax import lax
from jax.experimental import pallas as pl
from jax.experimental.pallas import tpu as pltpu
from jax.sharding import PartitionSpec as P

HEAD = 64


def extended(block, sides, width):
    for axis, dim in sides:
        count = lax.axis_size(axis)
        forward = [(i, i + 1) for i in range(count - 1)]
        backward = [(target, source) for source, target in forward]
        low = lax.ppermute(
            lax.slice_in_dim(block, block.shape[dim] - width, None, axis=dim), axis, forward
        )
        high = lax.ppermute(lax.slice_in_dim(block, 0, width, axis=dim), axis, backward)
        block = jnp.concatenate([low, block, high], axis=dim)
    return block


def temporal_conv(padded, w_temporal, b_temporal):
    count = padded.shape[0] - 2
    total = padded[1 : 1 + count].astype(jnp.float32) + b_temporal
    for tap in range(3):
        total = total + jnp.einsum(
            "frwc,co->frwo",
            padded[tap : tap + count],
            w_temporal[tap],
            preferred_element_type=jnp.float32,
        )
    return total.astype(jnp.bfloat16)


def attend_back(framed, ln_gain, ln_bias, w_query, w_key, w_value, w_out, b_out):
    frames, rows, cols, width = framed.shape
    values32 = framed.astype(jnp.float32)
    center = jnp.mean(values32, axis=-1, keepdims=True)
    spread = jnp.mean((values32 - center) ** 2, axis=-1, keepdims=True)
    normed = ((values32 - center) * lax.rsqrt(spread + 1e-05) * ln_gain + ln_bias).astype(
        jnp.bfloat16
    )
    query = jnp.einsum("frwc,cd->frwd", normed, w_query, preferred_element_type=jnp.float32).astype(
        jnp.bfloat16
    )
    key_rows = jnp.einsum(
        "frwc,cd->frwd", normed, w_key, preferred_element_type=jnp.float32
    ).astype(jnp.bfloat16)
    value = jnp.einsum("frwc,cd->frwd", normed, w_value, preferred_element_type=jnp.float32).astype(
        jnp.bfloat16
    )
    heads = width // HEAD
    query = query.reshape(frames, rows, cols, heads, HEAD)
    key_rows = key_rows.reshape(frames, rows, cols, heads, HEAD)
    value = value.reshape(frames, rows, cols, heads, HEAD)
    scores = jnp.einsum(
        "frwhd,grwhd->rwhfg", query, key_rows, preferred_element_type=jnp.float32
    ) / jnp.sqrt(jnp.float32(HEAD))
    top = jnp.max(scores, axis=-1, keepdims=True)
    raised = jnp.exp(scores - top)
    weights = (raised / jnp.sum(raised, axis=-1, keepdims=True)).astype(jnp.bfloat16)
    attended = jnp.einsum("rwhfg,grwhd->frwhd", weights, value, preferred_element_type=jnp.float32)
    attended = attended.reshape(frames, rows, cols, width).astype(jnp.bfloat16)
    result = (
        values32
        + jnp.einsum("frwc,co->frwo", attended, w_out, preferred_element_type=jnp.float32)
        + b_out
    )
    result = result.astype(jnp.bfloat16)
    return lax.all_to_all(result, "frame", split_axis=0, concat_axis=2, tiled=True)


def on_device(
    clip,
    w_spatial,
    b_spatial,
    w_temporal,
    b_temporal,
    ln_gain,
    ln_bias,
    w_query,
    w_key,
    w_value,
    w_out,
    b_out,
):
    rows = clip.shape[1]
    cols = clip.shape[2]
    padded = extended(clip, (("row", 1),), 1)
    padded = jnp.pad(padded, ((0, 0), (0, 0), (1, 1), (0, 0)))
    total = jnp.zeros(clip.shape, jnp.float32) + b_spatial
    for tap_row in range(3):
        for tap_col in range(3):
            window = padded[:, tap_row : tap_row + rows, tap_col : tap_col + cols]
            total = total + jnp.einsum(
                "frwc,co->frwo",
                window,
                w_spatial[tap_row, tap_col],
                preferred_element_type=jnp.float32,
            )
    spatial = total.astype(jnp.bfloat16)
    zero_rim = jnp.pad(
        lax.all_to_all(spatial, "frame", split_axis=2, concat_axis=0, tiled=True),
        ((1, 1), (0, 0), (0, 0), (0, 0)),
    )
    framed = temporal_conv(zero_rim, w_temporal, b_temporal)
    return attend_back(framed, ln_gain, ln_bias, w_query, w_key, w_value, w_out, b_out)


MESH = pl.DeviceIdType.MESH
F32 = jnp.float32
BF16 = jnp.bfloat16
PARTS = 4


def down(x, count):
    return jnp.concatenate([jnp.zeros((count, x.shape[1]), x.dtype), x[:-count]], axis=0)


def up(x, count):
    return jnp.concatenate([x[count:], jnp.zeros((count, x.shape[1]), x.dtype)], axis=0)


def dot(a, b):
    return jnp.dot(a, b, preferred_element_type=F32)


def fused(
    n, nrow, clip, wsp, wtp, wq, wk, wv, wo_in, vecs, out,
    ws, wt, wqkv, wo, xp, snd, rcv, osnd, orcv, load_sem, hsend, hrecv, s1, r1, s2, r2,
):
    me = lax.axis_index("frame")
    zi = lax.axis_index("row")
    rows = clip.shape[1]
    per = rows // PARTS
    above = lax.rem(zi + 1, nrow)
    below = lax.rem(zi + nrow - 1, nrow)

    load = pltpu.make_async_copy(clip, xp.at[:, pl.ds(1, rows)], load_sem)
    load.start()
    bs, bt, gain, lbias, bo = [vecs.at[pl.ds(i, 1)] for i in range(5)]

    barrier = pltpu.get_barrier_semaphore()

    def greet(k, _):
        pl.semaphore_signal(
            barrier, inc=1, device_id={"frame": lax.rem(me + k, n)}, device_id_type=MESH
        )
        return 0

    lax.fori_loop(1, n, greet, 0)
    pl.semaphore_signal(barrier, inc=1, device_id={"row": above}, device_id_type=MESH)
    pl.semaphore_signal(barrier, inc=1, device_id={"row": below}, device_id_type=MESH)
    pl.semaphore_wait(barrier, n + 1)

    to_above = pltpu.make_async_remote_copy(
        src_ref=clip.at[:, rows - 1], dst_ref=xp.at[:, 0],
        send_sem=hsend.at[0], recv_sem=hrecv.at[0],
        device_id={"row": above}, device_id_type=MESH,
    )
    to_below = pltpu.make_async_remote_copy(
        src_ref=clip.at[:, 0], dst_ref=xp.at[:, rows + 1],
        send_sem=hsend.at[1], recv_sem=hrecv.at[1],
        device_id={"row": below}, device_id_type=MESH,
    )
    to_above.start()
    to_below.start()

    def lay(target, first, count, parts):
        for b, w in enumerate(parts):
            target[first : first + count, 256 * b : 256 * b + 256] = w[:, :256]
        left = [w[:, 256:].astype(F32) for w in parts]
        target[first : first + count, 768:896] = jnp.concatenate(left[:2], axis=1).astype(BF16)
        target[first : first + count, 896:960] = left[2].astype(BF16)

    width = wq.shape[0]
    for a in range(3):
        lay(ws, width * a, width, [wsp[a, b] for b in range(3)])
    lay(wt, 0, width, [wtp[k] for k in range(3)])
    scaled = (wq[...].astype(F32) * HEAD ** -0.5).astype(BF16)
    wqkv[:, :256] = scaled[:, :256]
    wqkv[:, 256:512] = wk[:, :256]
    wqkv[:, 512:768] = wv[:, :256]
    wqkv[:, 768:896] = jnp.concatenate(
        [scaled[:, 256:].astype(F32), jnp.zeros((width, 64), F32)], axis=1
    ).astype(BF16)
    wqkv[:, 896:1024] = jnp.concatenate(
        [wk[:, 256:].astype(F32), wv[:, 256:].astype(F32)], axis=1
    ).astype(BF16)
    wo[:256] = wo_in[:256]
    wo[256:320] = jnp.zeros((64, width), BF16)
    wo[320:] = wo_in[256:]
    load.wait()

    def move(buf, land, ss, rs, part, k):
        peer = lax.rem(me + k, n)
        span = pl.ds(part * per, per)
        return pltpu.make_async_remote_copy(
            src_ref=buf.at[peer, span], dst_ref=land.at[me, span],
            send_sem=ss.at[part, k], recv_sem=rs.at[part, k],
            device_id={"frame": peer}, device_id_type=MESH,
        )

    def arrived(buf, land, ss, rs, part, k):
        source = lax.rem(me + n - k, n)
        span = pl.ds(part * per, per)
        return pltpu.make_async_remote_copy(
            src_ref=buf.at[source, span], dst_ref=land.at[source, span],
            send_sem=ss.at[part, k], recv_sem=rs.at[part, k],
            device_id={"frame": source}, device_id_type=MESH,
        )

    def send_all(buf, land, ss, rs, part):
        def one(k, _):
            move(buf, land, ss, rs, part, k).start()
            return 0
        lax.fori_loop(1, n, one, 0)
        span = pl.ds(part * per, per)
        land[me, span] = buf[me, span]

    def recv_all(buf, land, ss, rs, part):
        def one(k, _):
            arrived(buf, land, ss, rs, part, k).wait_recv()
            return 0
        lax.fori_loop(1, n, one, 0)

    def drain(buf, land, ss, rs):
        def one(i, _):
            move(buf, land, ss, rs, i // (n - 1), 1 + i % (n - 1)).wait_send()
            return 0
        lax.fori_loop(0, PARTS * (n - 1), one, 0)

    def taps(y):
        main = [y[:, 256 * b : 256 * b + 256] for b in range(3)]
        left = [y[:, 768 + 64 * b : 832 + 64 * b] for b in range(3)]
        return main, left

    def conv_row(r):
        x = [xp[f, pl.ds(r, 3)].reshape(3 * width, 128).T for f in range(2)]
        y = dot(jnp.concatenate(x, axis=0), ws[...])
        pieces = []
        for f in range(2):
            main, left = taps(y[128 * f : 128 * f + 128])
            pieces.append([
                down(t[0], 1) + t[1] + up(t[2], 1) + b
                for t, b in ((main, bs[...][:, :256]), (left, bs[...][:, 256:]))
            ])

        def grouped(values):
            width = values[0].shape[1]
            both = [v.reshape(n, 2, 1, 8, width) for v in values]
            return [
                jnp.concatenate([both[0][:, g], both[1][:, g]], axis=1).reshape(n, 16, width)
                for g in range(2)
            ]

        main = grouped([pieces[0][0], pieces[1][0]])
        left = grouped([pieces[0][1], pieces[1][1]])
        for g in range(2):
            for half in range(2):
                snd[:, r, 2 * g + half] = main[g][:, :, 128 * half : 128 * half + 128].astype(BF16)
        snd[:, r, 4] = jnp.concatenate(left, axis=2).astype(BF16)

    lane = lax.broadcasted_iota(jnp.int32, (1, 128), 1)
    low = lane < HEAD
    same = lax.broadcasted_iota(jnp.int32, (8, 128), 0) == lax.broadcasted_iota(
        jnp.int32, (8, 128), 1
    ) % 8
    wall = jnp.where(same, 0.0, -1e30).astype(F32)

    def attend_row(r):
        m = 16 * n
        rest = rcv[:, r, 4].reshape(m, 128).astype(F32)
        xs = []
        for g in range(2):
            a = rcv[:, r, 2 * g].reshape(m, 128).astype(F32)
            b = rcv[:, r, 2 * g + 1].reshape(m, 128).astype(F32)
            own = rest if g == 0 else pltpu.roll(rest, 64, 1)
            xs.append(jnp.concatenate([a, b, own[:, :64]], axis=1))
        x = jnp.concatenate(xs, axis=0)
        y = dot(x.astype(BF16), wt[...])
        sums = []
        for g in range(2):
            main, left = taps(y[m * g : m * g + m])
            sums.append(jnp.concatenate(
                [down(t[0], 8) + t[1] + up(t[2], 8) for t in (main, left)], axis=1
            ))
        framed = (x + bt[...] + jnp.concatenate(sums, axis=0)).astype(BF16).astype(F32)
        center = jnp.sum(framed, axis=1, keepdims=True) * (1.0 / framed.shape[1])
        away = framed - center
        spread = jnp.sum(away * away, axis=1, keepdims=True) * (1.0 / framed.shape[1])
        normed = (away * lax.rsqrt(spread + 1e-05) * gain[...] + lbias[...]).astype(BF16)
        qkv = dot(normed, wqkv[...])
        ones = jnp.ones((m, 128), BF16)
        rows_out = []
        for g in range(2):
            part = qkv[m * g : m * g + m]

            def head(q, k, v):
                s = lax.dot_general(
                    q.astype(BF16), k, (((1,), (1,)), ((), ())), preferred_element_type=F32
                )
                s = (s.reshape(m // 8, 8, m) + wall[None]).reshape(m, m)
                e = jnp.exp(s - jnp.max(s, axis=1, keepdims=True)).astype(BF16)
                return dot(e, jnp.concatenate([v, ones], axis=1))

            cols = []
            for j in range(2):
                q = part[:, 128 * j : 128 * j + 128]
                k = part[:, 256 + 128 * j : 384 + 128 * j].astype(BF16)
                v = part[:, 512 + 128 * j : 640 + 128 * j].astype(BF16)
                even = head(jnp.where(low, q, 0.0), k, v)
                odd = head(jnp.where(low, 0.0, q), k, v)
                cols.append(
                    (jnp.where(low, even[:, :128], odd[:, :128])
                     / jnp.where(low, even[:, 128:], odd[:, 128:])).astype(BF16)
                )
            kv = part[:, 896:1024].astype(BF16)
            last = head(part[:, 768:896], kv, kv)
            cols.append((last[:, :128] / last[:, 128:]).astype(BF16))
            rows_out.append(jnp.concatenate(cols, axis=1))
        result = framed + dot(jnp.concatenate(rows_out, axis=0), wo[...]) + bo[...]
        lefts = []
        for g in range(2):
            part = result[m * g : m * g + m]
            for half in range(2):
                osnd[:, r, 2 * g + half] = (
                    part[:, 128 * half : 128 * half + 128].astype(BF16).reshape(n, 16, 128)
                )
            lefts.append(part[:, 256:])
        osnd[:, r, 4] = jnp.concatenate(lefts, axis=1).astype(BF16).reshape(n, 16, 128)

    def unpack_row(r):
        def pair(first, second):
            a = first.reshape(n, 2, 8, 128)
            b = second.reshape(n, 2, 8, 128)
            return [
                jnp.concatenate([a[:, f : f + 1], b[:, f : f + 1]], axis=1).reshape(16 * n, 128)
                for f in range(2)
            ]

        block = [orcv[:, r, i].astype(F32).reshape(16 * n, 128) for i in range(5)]
        for half in range(2):
            for f, value in enumerate(pair(block[half], block[2 + half])):
                out[f, r, 128 * half : 128 * half + 128] = value.T.astype(BF16)
        for f, value in enumerate(pair(block[4], pltpu.roll(block[4], 64, 1))):
            out[f, r, 256:320] = value.T[:64].astype(BF16)

    def each_row(part, body):
        def one(i, _):
            body(part * per + i)
            return 0
        lax.fori_loop(0, per, one, 0)

    def conv_part(i, _):
        part = lax.rem(i + 1, PARTS)

        @pl.when(i == PARTS - 2)
        def _():
            to_above.wait()
            to_below.wait()

            @pl.when(zi == 0)
            def _():
                xp[:, 0] = jnp.zeros((2,) + xp.shape[2:], BF16)

            @pl.when(zi == nrow - 1)
            def _():
                xp[:, rows + 1] = jnp.zeros((2,) + xp.shape[2:], BF16)

        each_row(part, conv_row)
        send_all(snd, rcv, s1, r1, part)
        return 0

    lax.fori_loop(0, PARTS, conv_part, 0)

    def attend_part(i, _):
        part = lax.rem(i + 1, PARTS)
        recv_all(snd, rcv, s1, r1, part)
        each_row(part, attend_row)
        send_all(osnd, orcv, s2, r2, part)
        return 0

    lax.fori_loop(0, PARTS, attend_part, 0)

    def unpack_part(i, _):
        part = lax.rem(i + 1, PARTS)
        recv_all(osnd, orcv, s2, r2, part)
        each_row(part, unpack_row)
        return 0

    lax.fori_loop(0, PARTS, unpack_part, 0)
    drain(snd, rcv, s1, r1)
    drain(osnd, orcv, s2, r2)


def fused_call(
    n, nrow, clip, w_spatial, b_spatial, w_temporal, b_temporal,
    ln_gain, ln_bias, w_query, w_key, w_value, w_out, b_out,
):
    width = clip.shape[3]
    rows = clip.shape[1]
    turned = jnp.swapaxes(clip, 2, 3)
    vecs = jnp.stack([b_spatial, b_temporal, ln_gain, ln_bias, b_out])
    vmem = pl.BlockSpec(memory_space=pltpu.VMEM)
    box = pltpu.VMEM((n, rows, 5, 16, 128), BF16)
    sems = pltpu.SemaphoreType.DMA((PARTS, n))
    result = pl.pallas_call(
        functools.partial(fused, n, nrow),
        out_shape=jax.ShapeDtypeStruct(turned.shape, BF16),
        in_specs=[pl.BlockSpec(memory_space=pl.ANY)] + [vmem] * 7,
        out_specs=vmem,
        scratch_shapes=[
            pltpu.VMEM((3 * width, 3 * width), BF16),
            pltpu.VMEM((width, 3 * width), BF16),
            pltpu.VMEM((width, 3 * width + 64), BF16),
            pltpu.VMEM((width + 64, width), BF16),
            pltpu.VMEM((2, rows + 2) + turned.shape[2:], BF16),
            box, box, box, box,
            pltpu.SemaphoreType.DMA,
            pltpu.SemaphoreType.DMA((2,)),
            pltpu.SemaphoreType.DMA((2,)),
            sems, sems, sems, sems,
        ],
        compiler_params=pltpu.CompilerParams(
            collective_id=0, has_side_effects=True, vmem_limit_bytes=48 * 1024 * 1024
        ),
        cost_estimate=pl.CostEstimate(
            flops=2 * 16 * width * width * clip.size // width,
            bytes_accessed=4 * clip.size, transcendentals=0,
        ),
    )(
        turned, w_spatial, w_temporal, w_query, w_key, w_value, w_out, vecs,
    )
    return jnp.swapaxes(result, 2, 3)


def solution(mesh):
    n, nrow = mesh.shape["frame"], mesh.shape["row"]

    def body(clip, *weights):
        frames, rows, cols, width = clip.shape
        if (frames, cols, width, n) == (2, 128, 5 * HEAD, 8) and rows % PARTS == 0 and nrow > 2:
            return fused_call(n, nrow, clip, *weights)
        return on_device(clip, *weights)

    placed = (P("frame", "row", None, None), P(), P(), P(), P(), P(), P(), P(), P(), P(), P(), P())
    return jax.shard_map(
        body,
        mesh=mesh,
        in_specs=placed,
        out_specs=P("frame", "row", None, None),
        check_vma=False,
    )
```
